1024 devices in a mesh: row: 32 (over z_lo, core), col: 32 (over y, x, z_hi).
Axes of the slice: x: 4, y: 4, z: 32 (z_hi: 2, z_lo: 16; z = z_hi * 16 + z_lo), core: 2. Of those that a mesh axis runs over, the one named last changes fastest.
Arguments:
- a_tiles: bfloat16 [32, 640, 128, 128], P('row', 'col'), may hold values from -6 to 6
- a_where: int32 [32, 640], P('row', 'col'), may hold values from 0 to 63, as said below
- a_count: int32 [32, 32], P('row', 'col'), may hold values from 6 to 20, as said below
- b_tiles: bfloat16 [32, 960, 128, 128], P('row', 'col'), may hold values from -0.125 to 0.125
- b_where: int32 [32, 960], P('row', 'col'), may hold values from 0 to 95, as said below
- b_count: int32 [32, 32], P('row', 'col'), may hold values from 10 to 30, as said below
Outputs:
- c_slab: bfloat16 [16384, 24576], P('row', 'col')
The draws below stay inside these ranges and needn't reach their ends.
Inputs may be any that keep to these rules, and one draw needn't show every extreme that they name: `a_where`: within one device the positions of its 20 slots are distinct. `a_count`: some device has all 20 slots occupied in every draw. `b_where`: within one device the positions of its 30 slots are distinct. `b_count`: some device has all 30 slots occupied in every draw.
All inputs are finite; a program needn't handle non-finite values.
Results may differ from the reference program's by a relative error of at most 0.001.
Values may be sent and summed in bfloat16 or wider, within the bound.
No kernel may reach another device: no remote copies, remote signals or barrier semaphores. Data moves between devices by JAX's collectives and lax.ppermute only.
A program may use at most 32 MiB of HBM per device.

```python
import jax
import jax.numpy as jnp
from jax import lax

TILE = 128
MT = 4
KT = 16
NT = 6
SA = 20
SB = 30
N_ROW = 32
N_COL = 32


def draw_a_where(key, part):
    key = jax.random.fold_in(key, 11)
    keys = jax.random.split(key, N_ROW * N_COL)
    picked = jax.vmap(lambda k: jax.random.permutation(k, MT * KT)[:SA])(keys)
    return picked.reshape(N_ROW, N_COL * SA).astype(jnp.int32)


def draw_a_count(key, part):
    key = jax.random.fold_in(key, 12)
    first, second = jax.random.split(key)
    counts = jax.random.randint(first, (N_ROW * N_COL,), max(1, SA // 3), SA + 1)
    fullest = jax.random.randint(second, (), 0, N_ROW * N_COL)
    counts = counts.at[fullest].set(SA)
    return counts.reshape(N_ROW, N_COL).astype(jnp.int32)


def draw_b_where(key, part):
    key = jax.random.fold_in(key, 13)
    keys = jax.random.split(key, N_ROW * N_COL)
    picked = jax.vmap(lambda k: jax.random.permutation(k, KT * NT)[:SB])(keys)
    return picked.reshape(N_ROW, N_COL * SB).astype(jnp.int32)


def draw_b_count(key, part):
    key = jax.random.fold_in(key, 14)
    first, second = jax.random.split(key)
    counts = jax.random.randint(first, (N_ROW * N_COL,), max(1, SB // 3), SB + 1)
    fullest = jax.random.randint(second, (), 0, N_ROW * N_COL)
    counts = counts.at[fullest].set(SB)
    return counts.reshape(N_ROW, N_COL).astype(jnp.int32)


def shard_levels(rng, shape, cuts, low, top_value):
    def one(axis_at, blocks):
        steps = jax.random.uniform(jax.random.fold_in(jax.random.fold_in(rng, 6), axis_at), (blocks,), jnp.float32, low / len(cuts), top_value / len(cuts))
        return jnp.repeat(jnp.exp(steps), shape[axis_at] // blocks).reshape((-1,) + (1,) * (len(shape) - axis_at - 1))

    loudness = one(*cuts[0])
    for cut in cuts[1:]:
        loudness = loudness * one(*cut)
    return loudness


def gaussian(rng, shape, deviation, limit, shards=(), kind=jnp.bfloat16):
    result = deviation * jax.random.normal(rng, shape, jnp.float32)
    if shards:
        result = result * shard_levels(rng, shape, shards, -0.22, 0.18)
    return jnp.clip(result, -limit, limit).astype(kind)


def setup_inputs(seed: int = 0) -> dict:
    key_of = jax.random.split(jax.random.key(seed), 7)
    a_tiles = gaussian(key_of[0], (N_ROW, N_COL * SA, TILE, TILE), 1.0, 6.0, ((0, 32), (1, 32)))
    a_where = draw_a_where(jax.random.fold_in(key_of[6], 71), 0)
    a_count = draw_a_count(jax.random.fold_in(key_of[6], 71), 0)
    b_tiles = gaussian(key_of[3], (N_ROW, N_COL * SB, TILE, TILE), (KT * TILE) ** -0.5, 0.125, ((0, 32), (1, 32)))
    b_where = draw_b_where(jax.random.fold_in(key_of[6], 71), 0)
    b_count = draw_b_count(jax.random.fold_in(key_of[6], 71), 0)
    return {"a_tiles": a_tiles, "a_where": a_where, "a_count": a_count, "b_tiles": b_tiles, "b_where": b_where, "b_count": b_count}


def unpack(tiles, where, count, rows, cols):
    live = jnp.arange(tiles.shape[0]) < count
    spots = jnp.where(live, where, rows * cols).astype(jnp.int32)
    dense = jnp.zeros((rows * cols + 1, TILE, TILE), tiles.dtype).at[spots].set(tiles)[: rows * cols]
    return dense.reshape(rows, cols, TILE, TILE).transpose(0, 2, 1, 3).reshape(rows * TILE, cols * TILE)


def reference(a_tiles, a_where, a_count, b_tiles, b_where, b_count):
    left_all = a_tiles.reshape(N_ROW, N_COL, SA, TILE, TILE)
    left_pos = a_where.reshape(N_ROW, N_COL, SA)
    right_all = b_tiles.reshape(N_ROW, N_COL, SB, TILE, TILE)
    right_pos = b_where.reshape(N_ROW, N_COL, SB)

    def one_block(index):
        i = index // N_COL
        j = index % N_COL
        j_next = (j + 1) % N_COL
        i_next = (i + 1) % N_ROW
        left_here = unpack(left_all[i, j], left_pos[i, j], a_count[i, j], MT, KT).astype(jnp.float32)
        left_next = unpack(left_all[i, j_next], left_pos[i, j_next], a_count[i, j_next], MT, KT).astype(jnp.float32)
        right_here = unpack(right_all[i, j], right_pos[i, j], b_count[i, j], KT, NT).astype(jnp.float32)
        right_next = unpack(right_all[i_next, j], right_pos[i_next, j], b_count[i_next, j], KT, NT).astype(jnp.float32)
        total = jnp.dot(left_here, right_here, preferred_element_type=jnp.float32)
        total = total + jnp.dot(left_next, right_next, preferred_element_type=jnp.float32)
        return total.astype(jnp.bfloat16)

    blocks = lax.map(one_block, jnp.arange(N_ROW * N_COL, dtype=jnp.int32))
    blocks = blocks.reshape(N_ROW, N_COL, MT * TILE, NT * TILE).transpose(0, 2, 1, 3)
    return blocks.reshape(N_ROW * MT * TILE, N_COL * NT * TILE)
```

```python
import jax
import jax.numpy as jnp
from jax import lax
from jax.experimental import pallas as pl
from jax.experimental.pallas import tpu as pltpu
from jax.sharding import PartitionSpec as P

TILE = 128
MT = 4
KT = 16
NT = 6
STRIP = 256
VMEM_LIMIT = 40 * 1024 * 1024


def passed_along(array, axis, by):
    size = lax.axis_size(axis)
    return lax.ppermute(array, axis, [(i, (i + by) % size) for i in range(size)])


def place(tiles, spots, count, dense, cols):
    dense[...] = jnp.zeros_like(dense)

    @pl.loop(0, count)
    def _(slot):
        spot = spots[0, slot]
        row = pl.multiple_of((spot // cols) * TILE, TILE)
        col = pl.multiple_of((spot % cols) * TILE, TILE)
        dense[pl.ds(row, TILE), pl.ds(col, TILE)] = tiles[slot]


def first_kernel(a_spots, a_count, b_spots, b_count, a_tiles, b_tiles, total, a_meta, b_meta, left, right):
    for spots, count, meta in ((a_spots, a_count, a_meta), (b_spots, b_count, b_meta)):
        slots = spots.shape[1]

        @pl.loop(0, slots)
        def _(slot):
            meta[0, slot] = spots[0, slot]

        meta[0, slots] = count[0, 0]
    place(a_tiles, a_spots, a_count[0, 0], left, KT)
    place(b_tiles, b_spots, b_count[0, 0], right, NT)
    for strip in range(0, NT * TILE, STRIP):
        cols = pl.ds(strip, STRIP)
        total[:, cols] = jnp.dot(left[...], right[:, cols], preferred_element_type=jnp.float32)


def place_kernel(b_meta, b_tiles, right):
    place(b_tiles, b_meta, b_meta[0, b_tiles.shape[0]], right, NT)


def last_kernel(a_meta, a_tiles, right, total, out, left):
    @pl.when(pl.program_id(0) == 0)
    def _():
        place(a_tiles, a_meta, a_meta[0, a_tiles.shape[0]], left, KT)

    added = jnp.dot(left[...], right[...], preferred_element_type=jnp.float32)
    out[...] = (total[...] + added).astype(out.dtype)


def shards(a_tiles, a_where, a_count, b_tiles, b_where, b_count):
    a_tiles, b_tiles = a_tiles[0], b_tiles[0]
    slots_a, slots_b = a_tiles.shape[0], b_tiles.shape[0]
    rows, depth, cols = MT * TILE, KT * TILE, NT * TILE
    smem = pl.BlockSpec(memory_space=pltpu.SMEM)
    vmem = pl.BlockSpec(memory_space=pltpu.VMEM)
    params = pltpu.CompilerParams(vmem_limit_bytes=VMEM_LIMIT)
    macs = rows * depth * cols

    b_next = passed_along(b_tiles, "row", -1)
    a_next = passed_along(a_tiles, "col", -1)

    total, a_meta, b_meta = pl.pallas_call(
        first_kernel,
        out_shape=(
            jax.ShapeDtypeStruct((rows, cols), jnp.float32),
            jax.ShapeDtypeStruct((1, slots_a + 1), jnp.int32),
            jax.ShapeDtypeStruct((1, slots_b + 1), jnp.int32),
        ),
        in_specs=[smem, smem, smem, smem, vmem, vmem],
        out_specs=(vmem, smem, smem),
        scratch_shapes=[
            pltpu.VMEM((rows, depth), jnp.bfloat16),
            pltpu.VMEM((depth, cols), jnp.bfloat16),
        ],
        compiler_params=params,
        cost_estimate=pl.CostEstimate(flops=2 * macs, bytes_accessed=8 << 20, transcendentals=0),
    )(a_where, a_count, b_where, b_count, a_tiles, b_tiles)

    a_meta = passed_along(a_meta, "col", -1)
    b_meta = passed_along(b_meta, "row", -1)

    right = pl.pallas_call(
        place_kernel,
        out_shape=jax.ShapeDtypeStruct((depth, cols), jnp.bfloat16),
        in_specs=[smem, vmem],
        out_specs=vmem,
        compiler_params=params,
        cost_estimate=pl.CostEstimate(flops=0, bytes_accessed=8 << 20, transcendentals=0),
    )(b_meta, b_next)

    return pl.pallas_call(
        last_kernel,
        grid=(cols // STRIP,),
        out_shape=jax.ShapeDtypeStruct((rows, cols), jnp.bfloat16),
        in_specs=[
            smem,
            pl.BlockSpec((slots_a, TILE, TILE), lambda n: (0, 0, 0)),
            pl.BlockSpec((depth, STRIP), lambda n: (0, n)),
            pl.BlockSpec((rows, STRIP), lambda n: (0, n)),
        ],
        out_specs=pl.BlockSpec((rows, STRIP), lambda n: (0, n)),
        scratch_shapes=[pltpu.VMEM((rows, depth), jnp.bfloat16)],
        compiler_params=params,
        cost_estimate=pl.CostEstimate(flops=2 * macs, bytes_accessed=8 << 20, transcendentals=0),
    )(a_meta, a_next, right, total)


def solution(mesh):
    in_specs = (
        P("row", "col", None, None),
        P("row", "col"),
        P("row", "col"),
        P("row", "col", None, None),
        P("row", "col"),
        P("row", "col"),
    )
    out_specs = P("row", "col")
    return jax.shard_map(shards, mesh=mesh, in_specs=in_specs, out_specs=out_specs, check_vma=False)
```

```python
import jax
import jax.numpy as jnp
from jax import lax
from jax.experimental import pallas as pl
from jax.experimental.pallas import tpu as pltpu
from jax.sharding import PartitionSpec as P

TILE = 128
MT = 4
KT = 16
NT = 6
STRIP = 256
VMEM_LIMIT = 24 * 1024 * 1024


def passed_along(array, axis, by):
    size = lax.axis_size(axis)
    return lax.ppermute(array, axis, [(i, (i + by) % size) for i in range(size)])


def place(tiles, spots, count, dense, cols):
    dense[...] = jnp.zeros_like(dense)

    @pl.loop(0, count)
    def _(slot):
        spot = spots[0, slot]
        row = pl.multiple_of((spot // cols) * TILE, TILE)
        col = pl.multiple_of((spot % cols) * TILE, TILE)
        dense[pl.ds(row, TILE), pl.ds(col, TILE)] = tiles[slot]


def first_kernel(a_spots, a_count, b_spots, b_count, a_tiles, b_tiles, total, a_meta, b_meta, left, right):
    for spots, count, meta in ((a_spots, a_count, a_meta), (b_spots, b_count, b_meta)):
        slots = spots.shape[1]

        @pl.loop(0, slots)
        def _(slot):
            meta[0, slot] = spots[0, slot]

        meta[0, slots] = count[0, 0]
    place(a_tiles, a_spots, a_count[0, 0], left, KT)
    place(b_tiles, b_spots, b_count[0, 0], right, NT)
    for strip in range(0, NT * TILE, STRIP):
        cols = pl.ds(strip, STRIP)
        total[:, cols] = jnp.dot(left[...], right[:, cols], preferred_element_type=jnp.float32)


def place_kernel(b_meta, b_tiles, right):
    place(b_tiles, b_meta, b_meta[0, b_tiles.shape[0]], right, NT)


def last_kernel(a_meta, a_tiles, right, total, out, left):
    place(a_tiles, a_meta, a_meta[0, a_tiles.shape[0]], left, KT)
    for strip in range(0, NT * TILE, STRIP):
        cols = pl.ds(strip, STRIP)
        added = jnp.dot(left[...], right[:, cols], preferred_element_type=jnp.float32)
        out[:, cols] = (total[:, cols] + added).astype(out.dtype)


def shards(a_tiles, a_where, a_count, b_tiles, b_where, b_count):
    a_tiles, b_tiles = a_tiles[0], b_tiles[0]
    slots_a, slots_b = a_tiles.shape[0], b_tiles.shape[0]
    rows, depth, cols = MT * TILE, KT * TILE, NT * TILE
    smem = pl.BlockSpec(memory_space=pltpu.SMEM)
    vmem = pl.BlockSpec(memory_space=pltpu.VMEM)
    params = pltpu.CompilerParams(vmem_limit_bytes=VMEM_LIMIT)
    macs = rows * depth * cols

    b_next = passed_along(b_tiles, "row", -1)
    a_next = passed_along(a_tiles, "col", -1)

    total, a_meta, b_meta = pl.pallas_call(
        first_kernel,
        out_shape=(
            jax.ShapeDtypeStruct((rows, cols), jnp.float32),
            jax.ShapeDtypeStruct((1, slots_a + 1), jnp.int32),
            jax.ShapeDtypeStruct((1, slots_b + 1), jnp.int32),
        ),
        in_specs=[smem, smem, smem, smem, vmem, vmem],
        out_specs=(vmem, smem, smem),
        scratch_shapes=[
            pltpu.VMEM((rows, depth), jnp.bfloat16),
            pltpu.VMEM((depth, cols), jnp.bfloat16),
        ],
        compiler_params=params,
        cost_estimate=pl.CostEstimate(flops=2 * macs, bytes_accessed=8 << 20, transcendentals=0),
    )(a_where, a_count, b_where, b_count, a_tiles, b_tiles)

    a_meta = passed_along(a_meta, "col", -1)
    b_meta = passed_along(b_meta, "row", -1)

    right = pl.pallas_call(
        place_kernel,
        out_shape=jax.ShapeDtypeStruct((depth, cols), jnp.bfloat16),
        in_specs=[smem, vmem],
        out_specs=vmem,
        compiler_params=params,
        cost_estimate=pl.CostEstimate(flops=0, bytes_accessed=8 << 20, transcendentals=0),
    )(b_meta, b_next)

    return pl.pallas_call(
        last_kernel,
        out_shape=jax.ShapeDtypeStruct((rows, cols), jnp.bfloat16),
        in_specs=[smem, vmem, vmem, vmem],
        out_specs=vmem,
        scratch_shapes=[pltpu.VMEM((rows, depth), jnp.bfloat16)],
        compiler_params=params,
        cost_estimate=pl.CostEstimate(flops=2 * macs, bytes_accessed=8 << 20, transcendentals=0),
    )(a_meta, a_next, right, total)


def solution(mesh):
    in_specs = (
        P("row", "col", None, None),
        P("row", "col"),
        P("row", "col"),
        P("row", "col", None, None),
        P("row", "col"),
        P("row", "col"),
    )
    out_specs = P("row", "col")
    return jax.shard_map(shards, mesh=mesh, in_specs=in_specs, out_specs=out_specs, check_vma=False)
```

```python
import jax
import jax.numpy as jnp
from jax import lax
from jax.experimental import pallas as pl
from jax.experimental.pallas import tpu as pltpu
from jax.sharding import PartitionSpec as P

TILE = 128
MT = 4
KT = 16
NT = 6
STRIP = 256
VMEM_LIMIT = 24 * 1024 * 1024


def passed_along(array, axis, by):
    size = lax.axis_size(axis)
    return lax.ppermute(array, axis, [(i, (i + by) % size) for i in range(size)])


def place(tiles, spots, count, dense, cols):
    dense[...] = jnp.zeros_like(dense)

    @pl.loop(0, count)
    def _(slot):
        spot = spots[0, slot]
        row = pl.multiple_of((spot // cols) * TILE, TILE)
        col = pl.multiple_of((spot % cols) * TILE, TILE)
        dense[pl.ds(row, TILE), pl.ds(col, TILE)] = tiles[slot]


def first_kernel(a_spots, a_count, b_spots, b_count, a_tiles, b_tiles, total, a_meta, b_meta, left, right):
    for spots, count, meta in ((a_spots, a_count, a_meta), (b_spots, b_count, b_meta)):
        slots = spots.shape[1]

        @pl.loop(0, slots)
        def _(slot):
            meta[0, slot] = spots[0, slot]

        meta[0, slots] = count[0, 0]
    place(a_tiles, a_spots, a_count[0, 0], left, KT)
    place(b_tiles, b_spots, b_count[0, 0], right, NT)
    for strip in range(0, NT * TILE, STRIP):
        cols = pl.ds(strip, STRIP)
        total[:, cols] = jnp.dot(left[...], right[:, cols], preferred_element_type=jnp.float32)


def place_kernel(b_meta, b_tiles, right):
    place(b_tiles, b_meta, b_meta[0, b_tiles.shape[0]], right, NT)


def last_kernel(a_meta, a_tiles, right, total, out, left, strips, sems):
    place(a_tiles, a_meta, a_meta[0, a_tiles.shape[0]], left, KT)
    copies = []
    for at in range(NT * TILE // STRIP):
        cols = pl.ds(at * STRIP, STRIP)
        added = jnp.dot(left[...], right[:, cols], preferred_element_type=jnp.float32)
        strips[at] = (total[:, cols] + added).astype(out.dtype)
        copies.append(pltpu.make_async_copy(strips.at[at], out.at[:, cols], sems.at[at]))
        copies[-1].start()
    for copy in copies:
        copy.wait()


def shards(a_tiles, a_where, a_count, b_tiles, b_where, b_count):
    a_tiles, b_tiles = a_tiles[0], b_tiles[0]
    slots_a, slots_b = a_tiles.shape[0], b_tiles.shape[0]
    rows, depth, cols = MT * TILE, KT * TILE, NT * TILE
    smem = pl.BlockSpec(memory_space=pltpu.SMEM)
    vmem = pl.BlockSpec(memory_space=pltpu.VMEM)
    params = pltpu.CompilerParams(vmem_limit_bytes=VMEM_LIMIT)
    macs = rows * depth * cols

    b_next = passed_along(b_tiles, "row", -1)
    a_next = passed_along(a_tiles, "col", -1)

    total, a_meta, b_meta = pl.pallas_call(
        first_kernel,
        out_shape=(
            jax.ShapeDtypeStruct((rows, cols), jnp.float32),
            jax.ShapeDtypeStruct((1, slots_a + 1), jnp.int32),
            jax.ShapeDtypeStruct((1, slots_b + 1), jnp.int32),
        ),
        in_specs=[smem, smem, smem, smem, vmem, vmem],
        out_specs=(vmem, smem, smem),
        scratch_shapes=[
            pltpu.VMEM((rows, depth), jnp.bfloat16),
            pltpu.VMEM((depth, cols), jnp.bfloat16),
        ],
        compiler_params=params,
        cost_estimate=pl.CostEstimate(flops=2 * macs, bytes_accessed=8 << 20, transcendentals=0),
    )(a_where, a_count, b_where, b_count, a_tiles, b_tiles)

    a_meta = passed_along(a_meta, "col", -1)
    b_meta = passed_along(b_meta, "row", -1)

    right = pl.pallas_call(
        place_kernel,
        out_shape=jax.ShapeDtypeStruct((depth, cols), jnp.bfloat16),
        in_specs=[smem, vmem],
        out_specs=vmem,
        compiler_params=params,
        cost_estimate=pl.CostEstimate(flops=0, bytes_accessed=8 << 20, transcendentals=0),
    )(b_meta, b_next)

    return pl.pallas_call(
        last_kernel,
        out_shape=jax.ShapeDtypeStruct((rows, cols), jnp.bfloat16),
        in_specs=[smem, vmem, vmem, vmem],
        out_specs=pl.BlockSpec(memory_space=pl.ANY),
        scratch_shapes=[
            pltpu.VMEM((rows, depth), jnp.bfloat16),
            pltpu.VMEM((cols // STRIP, rows, STRIP), jnp.bfloat16),
            pltpu.SemaphoreType.DMA((cols // STRIP,)),
        ],
        compiler_params=params,
        cost_estimate=pl.CostEstimate(flops=2 * macs, bytes_accessed=8 << 20, transcendentals=0),
    )(a_meta, a_next, right, total)


def solution(mesh):
    in_specs = (
        P("row", "col", None, None),
        P("row", "col"),
        P("row", "col"),
        P("row", "col", None, None),
        P("row", "col"),
        P("row", "col"),
    )
    out_specs = P("row", "col")
    return jax.shard_map(shards, mesh=mesh, in_specs=in_specs, out_specs=out_specs, check_vma=False)
```
